32 devices in a mesh: freq: 2 (over y), bfly: 16 (over z, x, core).
Axes of the slice: x: 2, y: 2, z: 4, core: 2. Of those that a mesh axis runs over, the one named last changes fastest.
Arguments:
- coefficients: bfloat16 [32768, 512], P(('freq', 'bfly')), parts along dimension 0, may hold values from -6 to 6
- transfer: bfloat16 [5, 32768, 1024], P(None, ('freq', 'bfly')), parts along dimension 1, may hold values from -0.25 to 0.25
- ranks: int32 [6, 16], P(None, 'bfly'), may hold values from 256 to 1024, as said below
- owner_map: int32 [16], replicated, may hold values from 0 to 3, as said below
Outputs:
- target_field: bfloat16 [8192, 512], P(('freq', 'bfly')), parts along dimension 0
The draws below stay inside these ranges and needn't reach their ends.
There are 2 independent parts, one for each index of `freq`. The reference program is written for one: setup_inputs(seed, part) draws one part's arguments, and reference() takes and returns one part's arrays. A program takes and returns all parts, laid end to end along the dimension named above; an argument that names none is the same for every part. Nothing has to cross between parts.
Inputs may be any that keep to these rules, and one draw needn't show every extreme that they name: Every row of ranks holds the value 1024 at least once. `owner_map`: within each aligned group of four blocks the four entries are a permutation of 0 to 3.
All inputs are finite; a program needn't handle non-finite values.
Results may differ from the reference program's by a relative error of at most 0.0095.
Values may be sent and summed in bfloat16 or wider, within the bound.
No kernel may reach another device: no remote copies, remote signals or barrier semaphores. Data moves between devices by JAX's collectives and lax.ppermute only.
A program may use at most 64 MiB of HBM per device.

```python
import jax
import jax.numpy as jnp
import numpy as np
from jax import lax

R = 1024
W = 512
LEVELS = 5
NB = 16


def draw_ranks(key, part):
    base_key = jax.random.fold_in(key, 11)
    first_key, second_key, third_key = jax.random.split(base_key, 3)
    values = jax.random.randint(first_key, (LEVELS + 1, NB), R // 4, R + 1)
    top_pos = jax.random.randint(second_key, (LEVELS + 1, 1), 0, NB)
    low_pos = jax.random.randint(third_key, (LEVELS + 1, 1), 0, NB)
    columns = jnp.arange(NB)[None, :]
    values = jnp.where(columns == low_pos, R // 4, values)
    values = jnp.where(columns == top_pos, R, values)
    return values.astype(jnp.int32)


def draw_owner_map(key, part):
    base_key = jax.random.fold_in(key, 23)
    group_keys = jax.random.split(base_key, NB // 4)
    orders = jax.vmap(lambda one_key: jax.random.permutation(one_key, 4))(group_keys)
    last_row = (orders[-1] - orders[-1, 3] + 4) % 4
    orders = orders.at[-1].set(last_row)
    return orders.reshape(NB).astype(jnp.int32)


def shard_levels(key, extent, shards, smallest, high):
    level = 1.0
    for axis_at, blocks in shards:
        heights = jax.random.uniform(jax.random.fold_in(jax.random.fold_in(key, 6), axis_at), (blocks,), jnp.float32, smallest / len(shards), high / len(shards))
        level = level * jnp.repeat(jnp.exp(heights), extent[axis_at] // blocks).reshape((-1,) + (1,) * (len(extent) - 1 - axis_at))
    return level


def bell_draw(own_key, extent, spread, limit, shards=(), kind=jnp.bfloat16):
    loudness = shard_levels(own_key, extent, shards, -0.22, 0.18) if shards else 1.0
    drawn = jax.random.normal(own_key, extent, jnp.float32) * spread * loudness
    return jnp.minimum(jnp.maximum(drawn, -limit), limit).astype(kind)


def setup_inputs(seed: int = 0, part: int = 0) -> dict:
    key_list = jax.random.split(jax.random.key(seed), 5)
    own_keys = jax.random.split(jax.random.fold_in(key_list[4], part), 5)
    coefficients = bell_draw(own_keys[0], (NB * R, W), 1.0, 6.0, ((0, 16),))
    transfer = bell_draw(own_keys[1], (LEVELS, NB * R, R), (R // 2) ** -0.5, 0.25, ((1, 16),))
    ranks = draw_ranks(jax.random.fold_in(key_list[4], 71), part)
    owner_map = draw_owner_map(jax.random.fold_in(key_list[4], 71), part)
    return {"coefficients": coefficients, "transfer": transfer, "ranks": ranks, "owner_map": owner_map}


def block_product(operands):
    return jnp.dot(operands[0], operands[1], preferred_element_type=jnp.float32)


def reference(coefficients, transfer, ranks, owner_map):
    half_rows = R // 2
    log_count = NB.bit_length() - 1
    row_ids = jnp.arange(R, dtype=jnp.int32)
    blocks = np.arange(NB)
    current = coefficients.reshape(NB, R, W)
    live = row_ids[None, :] < ranks[0][:, None]
    current = jnp.where(live[:, :, None], current, jnp.zeros((), jnp.bfloat16))
    for level_idx in range(LEVELS):
        bit_pos = (log_count - 1 - level_idx) % log_count
        which_half = (blocks >> bit_pos) & 1
        low_blocks = blocks & ~(1 << bit_pos)
        high_blocks = blocks | (1 << bit_pos)
        halves = current.reshape(NB, half_rows, 2, W).transpose(0, 2, 1, 3)
        lower_half = halves[low_blocks, which_half]
        upper_half = halves[high_blocks, which_half]
        stacked = jnp.concatenate([lower_half, upper_half], axis=1)
        matrices = transfer[level_idx].reshape(NB, R, R)
        product = lax.map(block_product, (matrices, stacked))
        keep_rows = row_ids[None, :] < ranks[level_idx + 1][:, None]
        current = jnp.where(keep_rows[:, :, None], product, jnp.float32(0.0)).astype(jnp.bfloat16)
    totals = current.astype(jnp.float32).reshape(NB // 4, 4, R, W).sum(axis=1)
    quarters = totals.reshape(NB // 4, 4, R // 4, W)
    owners = owner_map.reshape(NB // 4, 4)
    group_ids = jnp.arange(NB // 4, dtype=jnp.int32)
    picked = quarters[group_ids[:, None], owners]
    return picked.reshape(NB * R // 4, W).astype(jnp.bfloat16)
```

```python
import functools

import jax
import jax.numpy as jnp
from jax import lax
from jax.experimental import pallas as pl
from jax.experimental.pallas import tpu as pltpu
from jax.sharding import PartitionSpec as P

CHUNK = 128
TILES = 4
ANY = pl.BlockSpec(memory_space=pl.ANY)
VMEM = pl.BlockSpec(memory_space=pltpu.VMEM)
SMEM = pl.BlockSpec(memory_space=pltpu.SMEM)
PARAMS = pltpu.CompilerParams(vmem_limit_bytes=8 * 1024 * 1024)


def from_partner(value, axis, apart):
    mask = 2**apart
    pairs = [(source, source ^ mask) for source in range(lax.axis_size(axis))]
    return lax.ppermute(value, axis, pairs)


def bit_of(apart):
    return lax.axis_index("bfly") >> apart & 1


def split_rows(values, first_row, ranks, level, half, y, own, other, base):
    rows, width = values.shape
    ids = lax.broadcasted_iota(jnp.int32, (rows, width), 0) + first_row
    y[...] = jnp.where(ids < ranks[level], values, 0.0)
    out = pl.ds(base, rows // 2)
    own[out, :] = y[pl.ds(half, rows // 2, stride=2), :].astype(jnp.bfloat16)
    other[out, :] = y[pl.ds(1 - half, rows // 2, stride=2), :].astype(jnp.bfloat16)


def first_kernel(apart, ranks, x, own, other, y):
    rows = x.shape[0] // TILES
    half = bit_of(apart)
    for tile in range(TILES):
        values = x[pl.ds(tile * rows, rows), :].astype(jnp.float32)
        split_rows(values, tile * rows, ranks, 0, half, y.at[tile], own, other, tile * rows // 2)


def stack_halves(apart, own, received, z):
    half_rows = own.shape[0]
    half = bit_of(apart)
    z[pl.ds(pl.multiple_of(half * half_rows, half_rows), half_rows), :] = own[...]
    z[pl.ds(pl.multiple_of((1 - half) * half_rows, half_rows), half_rows), :] = received[...]


def level_kernel(level, apart, next_apart, ranks, transfer, own, received, next_own, next_other, z, y):
    stack_halves(apart, own, received, z)
    rows = transfer.shape[1] // TILES
    half = bit_of(next_apart)
    for tile in range(TILES):
        matrix = transfer[level, pl.ds(tile * rows, rows), :]
        values = jnp.dot(matrix, z[...], preferred_element_type=jnp.float32)
        split_rows(values, tile * rows, ranks, level + 1, half, y.at[tile], next_own, next_other, tile * rows // 2)


def last_kernel(level, apart, ranks, owners, transfer, own, received, kept, sent, z, x):
    stack_halves(apart, own, received, z)
    rows = transfer.shape[1] // 4
    for tile in range(4):
        matrix = transfer[level, pl.ds(tile * rows, rows), :]
        values = jnp.dot(matrix, z[...], preferred_element_type=jnp.float32)
        ids = lax.broadcasted_iota(jnp.int32, values.shape, 0) + tile * rows
        x[pl.ds(tile * rows, rows), :] = jnp.where(ids < ranks[level + 1], values, 0.0).astype(jnp.bfloat16)
    position = lax.axis_index("bfly")
    for target, slot, flip in ((kept, 0, 0), (kept, 1, 2), (sent, 0, 1), (sent, 1, 3)):
        quarter = owners[position ^ flip]
        target[slot] = x[pl.ds(pl.multiple_of(quarter * rows, rows), rows), :]


def shape(*dims):
    return jax.ShapeDtypeStruct(dims, jnp.bfloat16)


def shards(coefficients, transfer, ranks, owner_map):
    rows, width = coefficients.shape
    levels = transfer.shape[0]
    ranks = ranks.reshape(-1)
    half, quarter = rows // 2, rows // 4
    count = lax.axis_size("bfly")
    log_count = count.bit_length() - 1
    bits = [(log_count - 1 - level) % log_count for level in range(levels)]
    tiles = pltpu.VMEM((TILES, rows // TILES, CHUNK), jnp.float32)
    stacked = pltpu.VMEM((rows, CHUNK), jnp.bfloat16)
    kept_all, sums = [], []

    for chunk in range(width // CHUNK):
        own, other = pl.pallas_call(
            functools.partial(first_kernel, bits[0]),
            out_shape=[shape(half, CHUNK)] * 2,
            grid=(1,),
            in_specs=[SMEM, pl.BlockSpec((rows, CHUNK), functools.partial(lambda c, i: (0, c), chunk))],
            out_specs=[pl.BlockSpec((half, CHUNK), lambda i: (0, 0))] * 2,
            scratch_shapes=[tiles],
            compiler_params=PARAMS,
        )(ranks, coefficients)
        for level in range(levels):
            received = from_partner(other, "bfly", bits[level])
            cost = pl.CostEstimate(flops=2 * rows * rows * CHUNK, bytes_accessed=rows * rows * 2, transcendentals=0)
            if level + 1 < levels:
                own, other = pl.pallas_call(
                    functools.partial(level_kernel, level, bits[level], bits[level + 1]),
                    out_shape=[shape(half, CHUNK)] * 2,
                    in_specs=[SMEM, VMEM, VMEM, VMEM],
                    out_specs=[VMEM, VMEM],
                    scratch_shapes=[stacked, tiles],
                    cost_estimate=cost,
                    compiler_params=PARAMS,
                )(ranks, transfer, own, received)
            else:
                kept, sent = pl.pallas_call(
                    functools.partial(last_kernel, level, bits[level]),
                    out_shape=[shape(2, quarter, CHUNK)] * 2,
                    in_specs=[SMEM, SMEM, VMEM, VMEM, VMEM],
                    out_specs=[VMEM, VMEM],
                    scratch_shapes=[stacked, stacked],
                    cost_estimate=cost,
                    compiler_params=PARAMS,
                )(ranks, owner_map, transfer, own, received)
        arrived = from_partner(sent, "bfly", 0)
        partial_sum = kept.astype(jnp.float32) + arrived.astype(jnp.float32)
        far_sum = from_partner(partial_sum[1].astype(jnp.bfloat16), "bfly", 1)
        sums.append((partial_sum[0] + far_sum.astype(jnp.float32)).astype(jnp.bfloat16))
    return jnp.concatenate(sums, axis=1)


def solution(mesh):
    in_specs = (P(("freq", "bfly"), None), P(None, ("freq", "bfly"), None), P(None, "bfly"), P())
    out_specs = P(("freq", "bfly"), None)
    return jax.shard_map(shards, mesh=mesh, in_specs=in_specs, out_specs=out_specs, check_vma=False)
```

```python
import functools

import jax
import jax.numpy as jnp
from jax import lax
from jax.experimental import pallas as pl
from jax.experimental.pallas import tpu as pltpu
from jax.sharding import PartitionSpec as P

CHUNK = 128
SUB = 8
TILES = 4
AHEAD = 2
ORDER = (0, 10, 1, 30, 20, 11, 2, 21, 12, 31, 3, 22, 13, 4, 23, 32, 14, 5, 24, 33, 15, 34, 25, 35)
GROUPS = [[0, 1], [2], [3]]
PACE = (1.0, 1.4, 1.05, 0.8, 1.55)
ANY = pl.BlockSpec(memory_space=pl.ANY)
HBM = pl.BlockSpec(memory_space=pltpu.HBM)
VMEM = pl.BlockSpec(memory_space=pltpu.VMEM)
SMEM = pl.BlockSpec(memory_space=pltpu.SMEM)
COST = pl.CostEstimate(flops=1, bytes_accessed=1, transcendentals=0)
PARAMS = pltpu.CompilerParams(vmem_limit_bytes=8 * 1024 * 1024)


def from_partner(value, axis, apart):
    mask = 2**apart
    pairs = [(source, source ^ mask) for source in range(lax.axis_size(axis))]
    return lax.ppermute(value, axis, pairs)


def bit_of(apart):
    return lax.axis_index("bfly") >> apart & 1


def masked(values, first_row, rank):
    ids = lax.broadcasted_iota(jnp.int32, values.shape, 0) + first_row
    return jnp.where(ids < rank[0:1, :], values, 0.0)


def split_rows(values, y, half, own, other, base):
    rows = values.shape[0]
    y[...] = values
    out = pl.ds(base, rows // 2)
    own[out, :] = y[pl.ds(half, rows // 2, stride=2), :].astype(jnp.bfloat16)
    other[out, :] = y[pl.ds(1 - half, rows // 2, stride=2), :].astype(jnp.bfloat16)


def split_chunk(apart, rank, x, y, own, other):
    rows = x.shape[0] // TILES
    half = bit_of(apart)
    for tile in range(TILES):
        values = masked(x[pl.ds(tile * rows, rows), :].astype(jnp.float32), tile * rows, rank)
        split_rows(values, y.at[tile], half, own, other, tile * rows // 2)


def columns(ref, chunk):
    return ref.at[:, pl.ds(chunk * CHUNK, CHUNK)]


def first_kernel(apart, chunk, ranks, owners, coefficients, spread_ranks, spread_owners, own, other, rank_s, owner_s, x, y, sems):
    copies = [
        pltpu.make_async_copy(ranks, rank_s, sems.at[0]),
        pltpu.make_async_copy(owners, owner_s, sems.at[1]),
        pltpu.make_async_copy(columns(coefficients, chunk), x, sems.at[2]),
    ]
    for copy in copies:
        copy.start()
    for copy in copies:
        copy.wait()
    position = lax.axis_index("bfly")
    for level in range(spread_ranks.shape[0]):
        spread_ranks[level] = jnp.full((SUB, CHUNK), rank_s[level], jnp.int32)
    for flip in range(spread_owners.shape[0]):
        spread_owners[flip] = jnp.full((SUB, CHUNK), owner_s[position ^ flip], jnp.int32)
    split_chunk(apart, spread_ranks.at[0], x, y, own, other)


def load_kernel(coefficients, transfer, after, x, *refs):
    matrices, sems = refs[:-1], refs[-1]
    copies = [pltpu.make_async_copy(coefficients, x, sems.at[len(matrices)])]
    copies += [pltpu.make_async_copy(transfer.at[i], ref, sems.at[i]) for i, ref in enumerate(matrices)]
    for copy in copies:
        copy.start()
    for copy in copies:
        copy.wait()


def chunk_kernel(apart, chunk, spread_ranks, x, after, own, other, y):
    split_chunk(apart, spread_ranks.at[0], columns(x, chunk), y, own, other)


def product(matrix, tile, rows, apart, own, received):
    half_rows = own.shape[0]
    half = bit_of(apart)
    tile_rows = pl.ds(tile * rows, rows)
    own_cols = pl.ds(pl.multiple_of(half * half_rows, half_rows), half_rows)
    peer_cols = pl.ds(pl.multiple_of((1 - half) * half_rows, half_rows), half_rows)
    values = jnp.dot(matrix[tile_rows, own_cols], own[...], preferred_element_type=jnp.float32)
    return values + jnp.dot(matrix[tile_rows, peer_cols], received[...], preferred_element_type=jnp.float32)


def level_kernel(level, apart, next_apart, spread_ranks, matrix, own, received, after, next_own, next_other, y):
    rows = matrix.shape[0] // TILES
    half = bit_of(next_apart)
    for tile in range(TILES):
        values = product(matrix, tile, rows, apart, own, received)
        values = masked(values, tile * rows, spread_ranks.at[level + 1])
        split_rows(values, y.at[tile], half, next_own, next_other, tile * rows // 2)


def last_kernel(level, apart, place, spread_ranks, spread_owners, matrix, own, received, after, *refs):
    kept, sent = refs[-2:]
    rows = matrix.shape[0] // 4
    quarters = []
    for tile in range(4):
        values = product(matrix, tile, rows, apart, own, received)
        quarters.append(masked(values, tile * rows, spread_ranks.at[level + 1]))
    for target, slot, flip in ((sent, 0, 1), (sent, 1, 3), (kept, 0, 0), (kept, 1, 2)):
        owner = spread_owners[flip][0:1, :]
        picked = quarters[0]
        for tile in range(1, 4):
            picked = jnp.where(owner == tile, quarters[tile], picked)
        target[slot, place] = picked.astype(jnp.bfloat16)


def shape(*dims):
    return jax.ShapeDtypeStruct(dims, jnp.bfloat16)


def plan(chunks, levels):
    if ORDER and (chunks, levels) == (4, 5):
        return [(step // 10, step % 10 - 1) for step in ORDER]
    steps = [(0.1 * chunk if chunk < AHEAD else 1.01, chunk, -1) for chunk in range(chunks)]
    for chunk in range(chunks):
        at = float(chunk)
        for level in range(levels):
            at += PACE[min(level, len(PACE) - 1)]
            steps.append((at, chunk, level))
    return [step[1:] for step in sorted(steps)]


def shards(coefficients, transfer, ranks, owner_map):
    rows, width = coefficients.shape
    levels = transfer.shape[0]
    half, quarter = rows // 2, rows // 4
    count = lax.axis_size("bfly")
    log_count = count.bit_length() - 1
    bits = [(log_count - 1 - level) % log_count for level in range(levels)]
    chunks = width // CHUNK
    groups = GROUPS if chunks == 4 else [[chunk] for chunk in range(chunks)]
    group_of = {chunk: group for group in groups for chunk in group}
    strip = pltpu.VMEM((rows, CHUNK), jnp.bfloat16)
    tiles = pltpu.VMEM((TILES, rows // TILES, CHUNK), jnp.float32)
    in_hbm = functools.partial(pltpu.with_memory_space_constraint, memory_space=pltpu.HBM)
    coefficients, transfer = in_hbm(coefficients), in_hbm(transfer)

    spread_ranks, spread_owners, first_own, first_other = pl.pallas_call(
        functools.partial(first_kernel, bits[0], 0),
        out_shape=[jax.ShapeDtypeStruct((n, SUB, CHUNK), jnp.int32) for n in (levels + 1, 4)] + [shape(half, CHUNK)] * 2,
        in_specs=[HBM, HBM, HBM],
        out_specs=[VMEM] * 4,
        scratch_shapes=[
            pltpu.SMEM((levels + 1,), jnp.int32),
            pltpu.SMEM((count,), jnp.int32),
            strip,
            tiles,
            pltpu.SemaphoreType.DMA((3,)),
        ],
        cost_estimate=COST,
        compiler_params=PARAMS,
    )(in_hbm(ranks.reshape(-1)), in_hbm(owner_map), coefficients)
    x, *matrices = pl.pallas_call(
        load_kernel,
        out_shape=[shape(rows, width)] + [shape(rows, rows)] * levels,
        in_specs=[HBM, HBM, ANY],
        out_specs=[VMEM] * (levels + 1),
        scratch_shapes=[pltpu.SemaphoreType.DMA((levels + 1,))],
        cost_estimate=COST,
        compiler_params=PARAMS,
    )(coefficients, transfer, first_own)

    own, received = [None] * chunks, [None] * chunks
    ends, sums, done = {}, {}, set()
    after = x
    for chunk, level in plan(chunks, levels):
        if level + 1 < levels:
            if level < 0 and chunk == 0:
                own[chunk], other = first_own, first_other
            elif level < 0:
                own[chunk], other = pl.pallas_call(
                    functools.partial(chunk_kernel, bits[0], chunk),
                    out_shape=[shape(half, CHUNK)] * 2,
                    in_specs=[VMEM, VMEM, ANY],
                    out_specs=[VMEM, VMEM],
                    scratch_shapes=[tiles],
                    cost_estimate=COST,
                    compiler_params=PARAMS,
                )(spread_ranks, x, after)
                after = own[chunk]
            else:
                own[chunk], other = pl.pallas_call(
                    functools.partial(level_kernel, level, bits[level], bits[level + 1]),
                    out_shape=[shape(half, CHUNK)] * 2,
                    in_specs=[VMEM, VMEM, VMEM, VMEM, ANY],
                    out_specs=[VMEM, VMEM],
                    scratch_shapes=[tiles],
                    cost_estimate=COST,
                    compiler_params=PARAMS,
                )(spread_ranks, matrices[level], own[chunk], received[chunk], after)
                after = own[chunk]
            received[chunk] = from_partner(other, "bfly", bits[level + 1])
        else:
            group = group_of[chunk]
            held = ends.get(group[0], [])
            ends[group[0]] = kept, sent = pl.pallas_call(
                functools.partial(last_kernel, level, bits[level], group.index(chunk)),
                out_shape=[shape(2, len(group), quarter, CHUNK)] * 2,
                in_specs=[VMEM, VMEM, VMEM, VMEM, VMEM, ANY] + [ANY] * len(held),
                out_specs=[VMEM, VMEM],
                input_output_aliases={6 + i: i for i in range(len(held))},
                cost_estimate=COST,
                compiler_params=PARAMS,
            )(spread_ranks, spread_owners, matrices[level], own[chunk], received[chunk], after, *held)
            after = kept
            done.add(chunk)
            if done >= set(group):
                arrived = from_partner(sent, "bfly", 0)
                partial_sum = kept.astype(jnp.float32) + arrived.astype(jnp.float32)
                far_sum = from_partner(partial_sum[1].astype(jnp.bfloat16), "bfly", 1)
                total = (partial_sum[0] + far_sum.astype(jnp.float32)).astype(jnp.bfloat16)
                sums.update({member: total[i] for i, member in enumerate(group)})
    return jnp.concatenate([sums[chunk] for chunk in range(chunks)], axis=1)


def solution(mesh):
    in_specs = (P(("freq", "bfly"), None), P(None, ("freq", "bfly"), None), P(None, "bfly"), P())
    out_specs = P(("freq", "bfly"), None)
    return jax.shard_map(shards, mesh=mesh, in_specs=in_specs, out_specs=out_specs, check_vma=False)
```

```python
import functools

import jax
import jax.numpy as jnp
from jax import lax
from jax.experimental import pallas as pl
from jax.experimental.pallas import tpu as pltpu
from jax.sharding import PartitionSpec as P

CHUNK = 128
SUB = 8
TILES = 4
AHEAD = 2
ORDER = (0, 10, 1, 30, 20, 11, 2, 21, 12, 31, 3, 22, 13, 4, 23, 32, 14, 5, 24, 33, 15, 34, 25, 35)
GROUPS = [[0, 1], [2], [3]]
EARLY = (1, 2)
PACE = (1.0, 1.4, 1.05, 0.8, 1.55)
ANY = pl.BlockSpec(memory_space=pl.ANY)
HBM = pl.BlockSpec(memory_space=pltpu.HBM)
VMEM = pl.BlockSpec(memory_space=pltpu.VMEM)
SMEM = pl.BlockSpec(memory_space=pltpu.SMEM)
COST = pl.CostEstimate(flops=1, bytes_accessed=1, transcendentals=0)
PARAMS = pltpu.CompilerParams(vmem_limit_bytes=8 * 1024 * 1024)


def from_partner(value, axis, apart):
    mask = 2**apart
    pairs = [(source, source ^ mask) for source in range(lax.axis_size(axis))]
    return lax.ppermute(value, axis, pairs)


def bit_of(apart):
    return lax.axis_index("bfly") >> apart & 1


def masked(values, first_row, rank):
    ids = lax.broadcasted_iota(jnp.int32, values.shape, 0) + first_row
    return jnp.where(ids < rank[0:1, :], values, 0.0)


def split_rows(values, y, half, own, other, base):
    rows = values.shape[0]
    y[...] = values
    out = pl.ds(base, rows // 2)
    own[out, :] = y[pl.ds(half, rows // 2, stride=2), :].astype(jnp.bfloat16)
    other[out, :] = y[pl.ds(1 - half, rows // 2, stride=2), :].astype(jnp.bfloat16)


def split_chunk(apart, rank, x, y, own, other):
    rows = x.shape[0] // TILES
    half = bit_of(apart)
    for tile in range(TILES):
        values = masked(x[pl.ds(tile * rows, rows), :].astype(jnp.float32), tile * rows, rank)
        split_rows(values, y.at[tile], half, own, other, tile * rows // 2)


def columns(ref, chunk):
    return ref.at[:, pl.ds(chunk * CHUNK, CHUNK)]


def first_kernel(apart, chunk, ranks, owners, coefficients, spread_ranks, spread_owners, own, other, rank_s, owner_s, x, y, sems):
    copies = [
        pltpu.make_async_copy(ranks, rank_s, sems.at[0]),
        pltpu.make_async_copy(owners, owner_s, sems.at[1]),
        pltpu.make_async_copy(columns(coefficients, chunk), x, sems.at[2]),
    ]
    for copy in copies:
        copy.start()
    for copy in copies:
        copy.wait()
    position = lax.axis_index("bfly")
    for level in range(spread_ranks.shape[0]):
        spread_ranks[level] = jnp.full((SUB, CHUNK), rank_s[level], jnp.int32)
    for flip in range(spread_owners.shape[0]):
        spread_owners[flip] = jnp.full((SUB, CHUNK), owner_s[position ^ flip], jnp.int32)
    split_chunk(apart, spread_ranks.at[0], x, y, own, other)


def load_kernel(coefficients, transfer, after, x, *refs):
    matrices, sems = refs[:-1], refs[-1]
    copies = [pltpu.make_async_copy(coefficients, x, sems.at[len(matrices)])]
    copies += [pltpu.make_async_copy(transfer.at[i], ref, sems.at[i]) for i, ref in enumerate(matrices)]
    for copy in copies:
        copy.start()
    for copy in copies:
        copy.wait()


def chunk_kernel(apart, chunk, spread_ranks, x, after, own, other, y):
    split_chunk(apart, spread_ranks.at[0], columns(x, chunk), y, own, other)


def own_kernel(apart, matrix, own, after, total):
    half_rows = own.shape[0]
    own_cols = pl.ds(pl.multiple_of(bit_of(apart) * half_rows, half_rows), half_rows)
    total[...] = jnp.dot(matrix[:, own_cols], own[...], preferred_element_type=jnp.float32)


def product(matrix, tile, rows, apart, own, received):
    half_rows = received.shape[0]
    half = bit_of(apart)
    tile_rows = pl.ds(tile * rows, rows)
    own_cols = pl.ds(pl.multiple_of(half * half_rows, half_rows), half_rows)
    peer_cols = pl.ds(pl.multiple_of((1 - half) * half_rows, half_rows), half_rows)
    if own.dtype == jnp.float32:
        values = own[tile_rows, :]
    else:
        values = jnp.dot(matrix[tile_rows, own_cols], own[...], preferred_element_type=jnp.float32)
    return values + jnp.dot(matrix[tile_rows, peer_cols], received[...], preferred_element_type=jnp.float32)


def level_kernel(level, apart, next_apart, spread_ranks, matrix, own, received, after, next_own, next_other, y):
    rows = matrix.shape[0] // TILES
    half = bit_of(next_apart)
    for tile in range(TILES):
        values = product(matrix, tile, rows, apart, own, received)
        values = masked(values, tile * rows, spread_ranks.at[level + 1])
        split_rows(values, y.at[tile], half, next_own, next_other, tile * rows // 2)


def last_kernel(level, apart, place, spread_ranks, spread_owners, matrix, own, received, after, *refs):
    kept, sent = refs[-2:]
    rows = matrix.shape[0] // 4
    quarters = []
    for tile in range(4):
        values = product(matrix, tile, rows, apart, own, received)
        quarters.append(masked(values, tile * rows, spread_ranks.at[level + 1]))
    for target, slot, flip in ((sent, 0, 1), (sent, 1, 3), (kept, 0, 0), (kept, 1, 2)):
        owner = spread_owners[flip][0:1, :]
        picked = quarters[0]
        for tile in range(1, 4):
            picked = jnp.where(owner == tile, quarters[tile], picked)
        target[slot, place] = picked.astype(jnp.bfloat16)


def shape(*dims):
    return jax.ShapeDtypeStruct(dims, jnp.bfloat16)


def plan(chunks, levels):
    if ORDER and (chunks, levels) == (4, 5):
        return [(step // 10, step % 10 - 1) for step in ORDER]
    steps = [(0.1 * chunk if chunk < AHEAD else 1.01, chunk, -1) for chunk in range(chunks)]
    for chunk in range(chunks):
        at = float(chunk)
        for level in range(levels):
            at += PACE[min(level, len(PACE) - 1)]
            steps.append((at, chunk, level))
    return [step[1:] for step in sorted(steps)]


def shards(coefficients, transfer, ranks, owner_map):
    rows, width = coefficients.shape
    levels = transfer.shape[0]
    half, quarter = rows // 2, rows // 4
    count = lax.axis_size("bfly")
    log_count = count.bit_length() - 1
    bits = [(log_count - 1 - level) % log_count for level in range(levels)]
    chunks = width // CHUNK
    groups = GROUPS if chunks == 4 else [[chunk] for chunk in range(chunks)]
    group_of = {chunk: group for group in groups for chunk in group}
    strip = pltpu.VMEM((rows, CHUNK), jnp.bfloat16)
    tiles = pltpu.VMEM((TILES, rows // TILES, CHUNK), jnp.float32)
    in_hbm = functools.partial(pltpu.with_memory_space_constraint, memory_space=pltpu.HBM)
    coefficients, transfer = in_hbm(coefficients), in_hbm(transfer)

    spread_ranks, spread_owners, first_own, first_other = pl.pallas_call(
        functools.partial(first_kernel, bits[0], 0),
        out_shape=[jax.ShapeDtypeStruct((n, SUB, CHUNK), jnp.int32) for n in (levels + 1, 4)] + [shape(half, CHUNK)] * 2,
        in_specs=[HBM, HBM, HBM],
        out_specs=[VMEM] * 4,
        scratch_shapes=[
            pltpu.SMEM((levels + 1,), jnp.int32),
            pltpu.SMEM((count,), jnp.int32),
            strip,
            tiles,
            pltpu.SemaphoreType.DMA((3,)),
        ],
        cost_estimate=COST,
        compiler_params=PARAMS,
    )(in_hbm(ranks.reshape(-1)), in_hbm(owner_map), coefficients)
    x, *matrices = pl.pallas_call(
        load_kernel,
        out_shape=[shape(rows, width)] + [shape(rows, rows)] * levels,
        in_specs=[HBM, HBM, ANY],
        out_specs=[VMEM] * (levels + 1),
        scratch_shapes=[pltpu.SemaphoreType.DMA((levels + 1,))],
        cost_estimate=COST,
        compiler_params=PARAMS,
    )(coefficients, transfer, first_own)

    own, received = [None] * chunks, [None] * chunks
    ends, sums, done = {}, {}, set()
    after = x
    for chunk, level in plan(chunks, levels):
        if 10 * chunk + level + 1 in EARLY:
            own[chunk] = after = pl.pallas_call(
                functools.partial(own_kernel, bits[level]),
                out_shape=jax.ShapeDtypeStruct((rows, CHUNK), jnp.float32),
                in_specs=[VMEM, VMEM, ANY],
                out_specs=VMEM,
                cost_estimate=COST,
                compiler_params=PARAMS,
            )(matrices[level], own[chunk], after)
        if level + 1 < levels:
            if level < 0 and chunk == 0:
                own[chunk], other = first_own, first_other
            elif level < 0:
                own[chunk], other = pl.pallas_call(
                    functools.partial(chunk_kernel, bits[0], chunk),
                    out_shape=[shape(half, CHUNK)] * 2,
                    in_specs=[VMEM, VMEM, ANY],
                    out_specs=[VMEM, VMEM],
                    scratch_shapes=[tiles],
                    cost_estimate=COST,
                    compiler_params=PARAMS,
                )(spread_ranks, x, after)
                after = own[chunk]
            else:
                own[chunk], other = pl.pallas_call(
                    functools.partial(level_kernel, level, bits[level], bits[level + 1]),
                    out_shape=[shape(half, CHUNK)] * 2,
                    in_specs=[VMEM, VMEM, VMEM, VMEM, ANY],
                    out_specs=[VMEM, VMEM],
                    scratch_shapes=[tiles],
                    cost_estimate=COST,
                    compiler_params=PARAMS,
                )(spread_ranks, matrices[level], own[chunk], received[chunk], after)
                after = own[chunk]
            received[chunk] = from_partner(other, "bfly", bits[level + 1])
        else:
            group = group_of[chunk]
            held = ends.get(group[0], [])
            ends[group[0]] = kept, sent = pl.pallas_call(
                functools.partial(last_kernel, level, bits[level], group.index(chunk)),
                out_shape=[shape(2, len(group), quarter, CHUNK)] * 2,
                in_specs=[VMEM, VMEM, VMEM, VMEM, VMEM, ANY] + [ANY] * len(held),
                out_specs=[VMEM, VMEM],
                input_output_aliases={6 + i: i for i in range(len(held))},
                cost_estimate=COST,
                compiler_params=PARAMS,
            )(spread_ranks, spread_owners, matrices[level], own[chunk], received[chunk], after, *held)
            after = kept
            done.add(chunk)
            if done >= set(group):
                arrived = from_partner(sent, "bfly", 0)
                partial_sum = kept.astype(jnp.float32) + arrived.astype(jnp.float32)
                far_sum = from_partner(partial_sum[1].astype(jnp.bfloat16), "bfly", 1)
                total = (partial_sum[0] + far_sum.astype(jnp.float32)).astype(jnp.bfloat16)
                sums.update({member: total[i] for i, member in enumerate(group)})
    return jnp.concatenate([sums[chunk] for chunk in range(chunks)], axis=1)


def solution(mesh):
    in_specs = (P(("freq", "bfly"), None), P(None, ("freq", "bfly"), None), P(None, "bfly"), P())
    out_specs = P(("freq", "bfly"), None)
    return jax.shard_map(shards, mesh=mesh, in_specs=in_specs, out_specs=out_specs, check_vma=False)
```
